32 devices in a mesh: ctx: 8 (over z, y), head: 4 (over x, core).
Axes of the slice: x: 2, y: 2, z: 4, core: 2. Of those that a mesh axis runs over, the one named last changes fastest.
Arguments:
- queries: bfloat16 [1024, 16384], P('ctx', 'head'), may hold values from -50 to 50
- keys: bfloat16 [1024, 1024], P('ctx', 'head'), may hold values from -4 to 4
- values: bfloat16 [1024, 1024], P('ctx', 'head'), may hold values from -6 to 6
- lengths: int32 [10], replicated, may hold values from 1 to 192, 1024 in all
- first_block: int32 [8], replicated, may hold values from 0 to 7, as said below
Outputs:
- attended: bfloat16 [1024, 16384], P(('ctx', 'head'))
The draws below stay inside these ranges and needn't reach their ends.
Inputs may be any that keep to these rules, and one draw needn't show every extreme that they name: first_block[d] = (d + c) mod 8 for one c of the draw; index d of ctx holds the blocks first_block[d] and 15 - first_block[d] in that order.
All inputs are finite; a program needn't handle non-finite values.
Results may differ from the reference program's by a relative error of at most 0.004.
Values may be sent and summed in bfloat16 or wider, within the bound.
A program may use at most 64 MiB of HBM per device.

```python
import math
import jax
import jax.numpy as jnp
import numpy as np
from jax import lax

DH = 128
KVH = 8
QPG = 16
BLOCK = 64
HQ = 128
PAIRS = 8
SEQ = 1024
DOC_MAX = 192
NDOCS = 10


def pair_draw(key):
    key_base = jax.random.fold_in(key, 101)
    key_query = jax.random.fold_in(key, 103)
    keys_out = jnp.clip(jax.random.normal(key_base, (SEQ, KVH * DH), jnp.float32), -4.0, 4.0)
    queries_out = jnp.clip(jax.random.normal(key_query, (SEQ, HQ * DH), jnp.float32), -4.0, 4.0)
    return (queries_out, keys_out)


def draw_queries(key, part):
    return pair_draw(key)[0].astype(jnp.bfloat16)


def draw_keys(key, part):
    return pair_draw(key)[1].astype(jnp.bfloat16)


def draw_first_block(key, part):
    offset = jax.random.randint(jax.random.fold_in(key, 201), (), 0, PAIRS)
    return ((jnp.arange(PAIRS, dtype=jnp.int32) + offset) % PAIRS).astype(jnp.int32)


def steps_of(rng, shape, pieces, smallest, top_value):
    factor_of, own = 1.0, jax.random.fold_in(rng, 6)
    for dim, shards_of in pieces:
        heights = jnp.exp(jax.random.uniform(jax.random.fold_in(own, dim), (shards_of,), jnp.float32, smallest / len(pieces), top_value / len(pieces)))
        factor_of = factor_of * jnp.repeat(heights, shape[dim] // shards_of).reshape([-1 if axis == dim else 1 for axis in range(len(shape))])
    return factor_of


def profile(count, total, bound, slope):
    portions = [(1 << 20) // math.isqrt(standing ** slope) + 1 for standing in range(2, count + 1)]
    spare, counts = total - bound - (count - 1), [1] * (count - 1)
    while spare > 0:
        free = [i for i in range(count - 1) if counts[i] < bound]
        pool, left = sum([portions[i] for i in free]), spare
        for i in free:
            addition = min(bound - counts[i], max(1, left * portions[i] // pool), spare)
            counts[i] = counts[i] + addition
            spare = spare - addition
    return np.array([bound] + counts)


def uneven(own_key, amount, total, reach, skew):
    if amount == 2:
        one = jax.random.randint(own_key, (), max(1, total - reach), min(reach, total - 1) + 1)
        return jnp.stack([one, total - one])
    tallies = jnp.asarray(profile(amount, total, reach, skew), jnp.int32)
    twos = (amount - 1) // 2
    source_of, sink = tallies[1:1 + 2 * twos:2], tallies[2:2 + 2 * twos:2]
    margin = jnp.minimum(source_of - 1, reach - sink)
    passed = jax.random.randint(jax.random.fold_in(own_key, 1), (twos,), 0, 1 << 20) % (margin + 1)
    tallies = tallies.at[1:1 + 2 * twos:2].set(source_of - passed).at[2:2 + 2 * twos:2].set(sink + passed)
    return tallies[jax.random.permutation(jax.random.fold_in(own_key, 2), amount)]


def gaussian(stream_key, extent, scale, most, cuts=(), held_as=jnp.bfloat16):
    result = jax.random.normal(stream_key, extent, jnp.float32) * scale
    if len(cuts) > 0:
        result = steps_of(stream_key, extent, cuts, -0.22, 0.18) * result
    return jnp.clip(result, min=-most, max=most).astype(held_as)


def setup_inputs(seed: int = 0) -> dict:
    key_list = jax.random.split(jax.random.key(seed), 6)
    return {
        "queries": draw_queries(jax.random.fold_in(key_list[5], 71), 0),
        "keys": draw_keys(jax.random.fold_in(key_list[5], 71), 0),
        "values": gaussian(key_list[2], (SEQ, KVH * DH), 1.0, 6.0, ((0, 8), (1, 4))),
        "lengths": uneven(key_list[3], NDOCS, SEQ, DOC_MAX, 2).astype(jnp.int32),
        "first_block": draw_first_block(jax.random.fold_in(key_list[5], 71), 0),
    }


def positions(first_block):
    rows = jnp.arange(SEQ, dtype=jnp.int32)
    device = rows // (2 * BLOCK)
    offset = rows % (2 * BLOCK)
    leading = first_block[device]
    which = jnp.where(offset < BLOCK, leading, 2 * PAIRS - 1 - leading)
    return (which * BLOCK + offset % BLOCK).astype(jnp.int32)

def documents(lengths, where_at):
    ends = jnp.cumsum(lengths)
    return lax.optimization_barrier(jnp.sum((ends[None, :] <= where_at[:, None]).astype(jnp.int32), axis=1))

def reference(queries, keys, values, lengths, first_block):
    pos = positions(first_block)
    order = jnp.zeros((SEQ,), jnp.int32).at[pos].set(jnp.arange(SEQ, dtype=jnp.int32))
    sorted_q = queries[order]
    sorted_k = keys[order]
    sorted_v = values[order]
    doc_all = documents(lengths, jnp.arange(SEQ, dtype=jnp.int32))
    query_rows = 2 * BLOCK
    key_rows = query_rows + DOC_MAX
    scale = 1.0 / math.sqrt(DH)

    def one_block(index):
        q_start = (index * query_rows).astype(jnp.int32)
        k_start = jnp.clip(q_start - DOC_MAX, 0, SEQ - key_rows).astype(jnp.int32)
        q_part = lax.dynamic_slice_in_dim(sorted_q, q_start, query_rows, 0)
        k_part = lax.dynamic_slice_in_dim(sorted_k, k_start, key_rows, 0)
        v_part = lax.dynamic_slice_in_dim(sorted_v, k_start, key_rows, 0)
        q_four = q_part.reshape(query_rows, KVH, QPG, DH).astype(jnp.float32)
        k_three = k_part.reshape(key_rows, KVH, DH).astype(jnp.float32)
        v_three = v_part.reshape(key_rows, KVH, DH).astype(jnp.float32)
        scores = jnp.einsum('qhgd,khd->qhgk', q_four, k_three) * scale
        q_pos = q_start + jnp.arange(query_rows, dtype=jnp.int32)
        k_pos = k_start + jnp.arange(key_rows, dtype=jnp.int32)
        q_doc = lax.dynamic_slice_in_dim(doc_all, q_start, query_rows, 0)
        k_doc = lax.dynamic_slice_in_dim(doc_all, k_start, key_rows, 0)
        allowed = (k_doc[None, :] == q_doc[:, None]) & (k_pos[None, :] <= q_pos[:, None])
        gate = allowed[:, None, None, :]
        masked = jnp.where(gate, scores, -1e+30)
        maxima = lax.optimization_barrier(jnp.max(masked, axis=-1))
        expo = jnp.where(gate, jnp.exp(masked - maxima[..., None]), 0.0)
        totals = lax.optimization_barrier(jnp.sum(expo, axis=-1))
        weights = expo.astype(jnp.bfloat16).astype(jnp.float32)
        mixed = jnp.einsum('qhgk,khd->qhgd', weights, v_three) / totals[..., None]
        return mixed.reshape(query_rows, HQ * DH).astype(jnp.bfloat16)
    blocks = lax.map(one_block, jnp.arange(SEQ // query_rows, dtype=jnp.int32))
    in_order = blocks.reshape(SEQ, HQ * DH)
    return in_order[pos]
```

```python
import functools
import math

import jax
import jax.numpy as jnp
from jax import lax
from jax.experimental import pallas as pl
from jax.experimental.pallas import tpu as pltpu
from jax.sharding import PartitionSpec as P

DH = 128
LOWEST = -1e30
MESH = pl.DeviceIdType.MESH


def reach(devices):
    levels = 0
    for power in range(2, 6):
        levels += min(1, devices // 2**power)
    return (1 << levels) - 1


def kernel(
    pairs, heads, span, kv_local, per_group, chunk, tile,
    lengths_ref, first_ref, q_hbm, k_ref, v_ref, out_ref,
    q_buf, own, upper, windows, bias, obuf,
    q_sem, up_send, up_recv, down_send, down_recv, out_send, out_recv, self_sem,
):
    device = lax.axis_index("ctx")
    group = lax.axis_index("head")
    rows_here = q_buf.shape[0]
    block = rows_here // 2
    share = rows_here // heads
    dests = block // share
    chunks = per_group // chunk
    width = chunk * DH
    keys_seen = (span + 1) * block

    load_q = pltpu.make_async_copy(q_hbm, q_buf, q_sem)
    load_q.start()

    def around(step):
        return lax.rem(device + (step + pairs), pairs)

    def slot(back):
        return pl.ds((span - back) * block, block)

    barrier = pltpu.get_barrier_semaphore()
    for step in range(1, span + 1):
        pl.semaphore_signal(barrier, inc=1, device_id={"ctx": around(step)}, device_id_type=MESH)
        pl.semaphore_signal(barrier, inc=1, device_id={"ctx": around(-step)}, device_id_type=MESH)
    for step in range(1, heads):
        pl.semaphore_signal(
            barrier, inc=1, device_id={"head": lax.rem(group + step, heads)}, device_id_type=MESH
        )
    for h in range(kv_local):
        own[h, :, :DH] = k_ref[:, h * DH : (h + 1) * DH]
        own[h, :, DH:] = v_ref[:, h * DH : (h + 1) * DH]
    pl.semaphore_wait(barrier, 2 * span + heads - 1)

    def up_copy(h, step):
        return pltpu.make_async_remote_copy(
            src_ref=own.at[h, pl.ds(0, block)],
            dst_ref=windows.at[h, 0, slot(step)],
            send_sem=up_send.at[h, step - 1],
            recv_sem=up_recv.at[h, step - 1],
            device_id={"ctx": around(step)},
            device_id_type=MESH,
        )

    def down_copy(h, step):
        part = pl.ds(0, rows_here) if step < span else pl.ds(block, block)
        return pltpu.make_async_remote_copy(
            src_ref=own.at[h, part],
            dst_ref=upper.at[h, step - 1, part],
            send_sem=down_send.at[h, step - 1],
            recv_sem=down_recv.at[h, step - 1],
            device_id={"ctx": around(-step)},
            device_id_type=MESH,
        )

    for h in range(kv_local):
        for step in range(span, 0, -1):
            up_copy(h, step).start()
            down_copy(h, step).start()

    first = first_ref[device]
    shape = (block, keys_seen)
    offset = lax.broadcasted_iota(jnp.int32, shape, 0)
    place = lax.broadcasted_iota(jnp.int32, shape, 1)
    for which in range(2):
        at = first if which == 0 else 2 * pairs - 1 - first
        query_pos = at * block + offset
        key_pos = (at - span) * block + place
        begin = jnp.zeros(shape, jnp.int32)
        end = jnp.int32(0)
        for j in range(lengths_ref.shape[0]):
            end = end + lengths_ref[j]
            ends = jnp.full(shape, end, jnp.int32)
            begin = jnp.where(ends <= query_pos, ends, begin)
        allowed = (key_pos >= begin) & (key_pos <= query_pos)
        bias[which] = jnp.where(allowed, 0.0, LOWEST)
    for h in range(kv_local):
        windows[h, 0, slot(0)] = own[h, :block]
        windows[h, 1, slot(0)] = own[h, block:]

    def arrived(h):
        for step in range(1, span + 1):
            up_copy(h, step).wait_recv()
            down_copy(h, step).wait_recv()
        mine = jnp.full((block, 2 * DH), first, jnp.int32)
        for back in range(1, span + 1):
            piece = upper[h, back - 1, block:].astype(jnp.float32)
            for away in range(1 - back, back, 2):
                if away > 0:
                    other = upper[h, away - 1, :block]
                elif away == 0:
                    other = own[h, :block]
                else:
                    other = windows[h, 0, slot(-away)]
                holder = (2 * pairs - 1 - back - away) // 2
                piece = jnp.where(mine == holder, other.astype(jnp.float32), piece)
            windows[h, 1, slot(back)] = piece.astype(jnp.bfloat16)

    factor = math.log2(math.e) / math.sqrt(DH)

    def out_copy(step, dest, row, column, index):
        source = lax.rem(group, heads) * (kv_local * per_group * DH) + column
        return pltpu.make_async_remote_copy(
            src_ref=obuf.at[pl.ds(row, share), pl.ds(column, width)],
            dst_ref=out_ref.at[:, pl.ds(pl.multiple_of(source, DH), width)],
            send_sem=out_send.at[step, index],
            recv_sem=out_recv.at[step, index],
            device_id={"head": dest},
            device_id_type=MESH,
        )

    def self_copy(column, index):
        row = pl.multiple_of(group * share, share)
        target = group * (kv_local * per_group * DH) + column
        return pltpu.make_async_copy(
            obuf.at[pl.ds(row, share), pl.ds(column, width)],
            out_ref.at[:, pl.ds(pl.multiple_of(target, DH), width)],
            self_sem.at[index],
        )

    def attend(which, h, c):
        row = pl.multiple_of(which * block, block)
        column = pl.multiple_of((h * chunks + c) * width, width)
        key = windows[h, which, :, :DH]
        value = windows[h, which, :, DH:]
        gate = jnp.concatenate([bias[which]] * tile, axis=0)
        for part in range(chunk // tile):
            at = [column + (part * tile + i) * DH for i in range(tile)]
            query = jnp.concatenate(
                [q_buf[pl.ds(row, block), pl.ds(pl.multiple_of(a, DH), DH)] for a in at], axis=0
            )
            scores = gate + lax.dot_general(
                query, key, (((1,), (1,)), ((), ())), preferred_element_type=jnp.float32
            )
            highest = jnp.max(scores, axis=1, keepdims=True)
            expo = jnp.exp2((scores - highest) * factor)
            total = jnp.sum(expo, axis=1, keepdims=True)
            mixed = jnp.dot(
                expo.astype(jnp.bfloat16), value, preferred_element_type=jnp.float32
            )
            mixed = (mixed / total).astype(jnp.bfloat16)
            for i, a in enumerate(at):
                obuf[pl.ds(row, block), pl.ds(pl.multiple_of(a, DH), DH)] = mixed[
                    i * block : (i + 1) * block
                ]
        index = h * chunks + c
        for t in range(dests):
            dest = which * dests + t
            step = lax.rem(dest - group + heads, heads)

            @pl.when(step != 0)
            def _():
                spot = pl.multiple_of(dest * share, share)
                out_copy(step, dest, spot, column, index).start()

            @pl.when(step == 0)
            def _():
                self_copy(column, index).start()

    here = (group * share) // block
    load_q.wait()
    for turn in range(2):
        which = 1 - here if turn == 0 else here
        for h in range(kv_local):
            if turn == 0:
                arrived(h)

            @pl.loop(0, chunks)
            def _(c):
                attend(which, h, c)

    for h in range(kv_local):
        for step in range(1, span + 1):
            up_copy(h, step).wait_send()
            down_copy(h, step).wait_send()
    for index in range(kv_local * chunks):
        column = index * width
        self_copy(column, index).wait()
        for step in range(1, heads):
            dest = lax.rem(group + step, heads)
            spot = pl.multiple_of(dest * share, share)
            out_copy(step, dest, spot, column, index).wait_send()
            sender = lax.rem(group - step + heads, heads)
            target = sender * (kv_local * per_group * DH) + column
            pltpu.make_async_remote_copy(
                src_ref=obuf.at[pl.ds(spot, share), pl.ds(column, width)],
                dst_ref=out_ref.at[:, pl.ds(pl.multiple_of(target, DH), width)],
                send_sem=out_send.at[step, index],
                recv_sem=out_recv.at[step, index],
                device_id={"head": dest},
                device_id_type=MESH,
            ).wait_recv()


def shards(queries, keys, values, lengths, first_block):
    rows_here = queries.shape[0]
    block = rows_here // 2
    kv_local = keys.shape[1] // DH
    per_group = queries.shape[1] // (kv_local * DH)
    pairs = lax.axis_size("ctx")
    heads = lax.axis_size("head")
    span = reach(pairs)
    keys_seen = (span + 1) * block
    chunk = max(per_group // 2, 1)
    tile = max(1, min(chunk, 1024 // keys_seen))
    count = kv_local * (per_group // chunk)
    body = functools.partial(
        kernel, pairs, heads, span, kv_local, per_group, chunk, tile
    )
    vmem = pl.BlockSpec(memory_space=pltpu.VMEM)
    smem = pl.BlockSpec(memory_space=pltpu.SMEM)
    hbm = pl.BlockSpec(memory_space=pl.ANY)
    return pl.pallas_call(
        body,
        out_shape=jax.ShapeDtypeStruct(
            (rows_here // heads, queries.shape[1] * heads), jnp.bfloat16
        ),
        in_specs=[smem, smem, hbm, vmem, vmem],
        out_specs=hbm,
        scratch_shapes=[
            pltpu.VMEM(queries.shape, jnp.bfloat16),
            pltpu.VMEM((kv_local, rows_here, 2 * DH), jnp.bfloat16),
            pltpu.VMEM((kv_local, span, rows_here, 2 * DH), jnp.bfloat16),
            pltpu.VMEM((kv_local, 2, keys_seen, 2 * DH), jnp.bfloat16),
            pltpu.VMEM((2, block, keys_seen), jnp.float32),
            pltpu.VMEM(queries.shape, jnp.bfloat16),
            pltpu.SemaphoreType.DMA,
            pltpu.SemaphoreType.DMA((kv_local, span)),
            pltpu.SemaphoreType.DMA((kv_local, span)),
            pltpu.SemaphoreType.DMA((kv_local, span)),
            pltpu.SemaphoreType.DMA((kv_local, span)),
            pltpu.SemaphoreType.DMA((heads, count)),
            pltpu.SemaphoreType.DMA((heads, count)),
            pltpu.SemaphoreType.DMA((count,)),
        ],
        compiler_params=pltpu.CompilerParams(
            collective_id=0, has_side_effects=True, vmem_limit_bytes=32 * 2**20
        ),
    )(lengths, first_block, queries, keys, values)


def solution(mesh):
    in_specs = (P("ctx", "head"), P("ctx", "head"), P("ctx", "head"), P(), P())
    out_specs = P(("ctx", "head"), None)
    return jax.shard_map(shards, mesh=mesh, in_specs=in_specs, out_specs=out_specs, check_vma=False)
```

```python
import functools
import math

import jax
import jax.numpy as jnp
from jax import lax
from jax.experimental import pallas as pl
from jax.experimental.pallas import tpu as pltpu
from jax.sharding import PartitionSpec as P

DH = 128
LOWEST = -1e30
MESH = pl.DeviceIdType.MESH


def reach(devices):
    levels = 0
    for power in range(2, 6):
        levels += min(1, devices // 2**power)
    return (1 << levels) - 1


def kernel(
    pairs, heads, span, kv_local, per_group, chunk, tile,
    lengths_hbm, first_hbm, q_hbm, k_hbm, v_hbm, out_ref,
    lengths_ref, first_ref, k_ref, v_ref, in_sem,
    q_buf, own, upper, windows, bias, obuf,
    q_sem, up_send, up_recv, down_send, down_recv, out_send, out_recv, self_sem,
):
    device = lax.axis_index("ctx")
    group = lax.axis_index("head")
    rows_here = q_buf.shape[0]
    block = rows_here // 2
    share = rows_here // heads
    dests = block // share
    chunks = per_group // chunk
    width = chunk * DH
    keys_seen = (span + 1) * block

    loads = [
        pltpu.make_async_copy(source, target, in_sem.at[i])
        for i, (source, target) in enumerate(
            [(k_hbm, k_ref), (v_hbm, v_ref), (first_hbm, first_ref), (lengths_hbm, lengths_ref)]
        )
    ]
    for load in loads:
        load.start()
    load_q = pltpu.make_async_copy(q_hbm, q_buf, q_sem)
    load_q.start()

    def around(step):
        return lax.rem(device + (step + pairs), pairs)

    def slot(back):
        return pl.ds((span - back) * block, block)

    barrier = pltpu.get_barrier_semaphore()
    for step in range(1, span + 1):
        pl.semaphore_signal(barrier, inc=1, device_id={"ctx": around(step)}, device_id_type=MESH)
        pl.semaphore_signal(barrier, inc=1, device_id={"ctx": around(-step)}, device_id_type=MESH)
    for step in range(1, heads):
        pl.semaphore_signal(
            barrier, inc=1, device_id={"head": lax.rem(group + step, heads)}, device_id_type=MESH
        )
    for load in loads:
        load.wait()
    for h in range(kv_local):
        own[h, :, :DH] = k_ref[:, h * DH : (h + 1) * DH]
        own[h, :, DH:] = v_ref[:, h * DH : (h + 1) * DH]
    pl.semaphore_wait(barrier, 2 * span + heads - 1)

    def up_copy(h, step):
        return pltpu.make_async_remote_copy(
            src_ref=own.at[h, pl.ds(0, block)],
            dst_ref=windows.at[h, 0, slot(step)],
            send_sem=up_send.at[h, step - 1],
            recv_sem=up_recv.at[h, step - 1],
            device_id={"ctx": around(step)},
            device_id_type=MESH,
        )

    def down_copy(h, step):
        part = pl.ds(0, rows_here) if step < span else pl.ds(block, block)
        return pltpu.make_async_remote_copy(
            src_ref=own.at[h, part],
            dst_ref=upper.at[h, step - 1, part],
            send_sem=down_send.at[h, step - 1],
            recv_sem=down_recv.at[h, step - 1],
            device_id={"ctx": around(-step)},
            device_id_type=MESH,
        )

    for h in range(kv_local):
        for step in range(span, 0, -1):
            up_copy(h, step).start()
            down_copy(h, step).start()

    first = first_ref[device]
    shape = (block, keys_seen)
    offset = lax.broadcasted_iota(jnp.int32, shape, 0)
    place = lax.broadcasted_iota(jnp.int32, shape, 1)
    for which in range(2):
        at = first if which == 0 else 2 * pairs - 1 - first
        query_pos = at * block + offset
        key_pos = (at - span) * block + place
        begin = jnp.zeros(shape, jnp.int32)
        end = jnp.int32(0)
        for j in range(lengths_ref.shape[0]):
            end = end + lengths_ref[j]
            ends = jnp.full(shape, end, jnp.int32)
            begin = jnp.where(ends <= query_pos, ends, begin)
        allowed = (key_pos >= begin) & (key_pos <= query_pos)
        bias[which] = jnp.where(allowed, 0.0, LOWEST)
    for h in range(kv_local):
        windows[h, 0, slot(0)] = own[h, :block]
        windows[h, 1, slot(0)] = own[h, block:]

    def arrived(h):
        for step in range(1, span + 1):
            up_copy(h, step).wait_recv()
            down_copy(h, step).wait_recv()
        mine = jnp.full((block, 2 * DH), first, jnp.int32)
        for back in range(1, span + 1):
            piece = upper[h, back - 1, block:].astype(jnp.float32)
            for away in range(1 - back, back, 2):
                if away > 0:
                    other = upper[h, away - 1, :block]
                elif away == 0:
                    other = own[h, :block]
                else:
                    other = windows[h, 0, slot(-away)]
                holder = (2 * pairs - 1 - back - away) // 2
                piece = jnp.where(mine == holder, other.astype(jnp.float32), piece)
            windows[h, 1, slot(back)] = piece.astype(jnp.bfloat16)

    factor = math.log2(math.e) / math.sqrt(DH)

    def out_copy(step, dest, row, column, index):
        source = lax.rem(group, heads) * (kv_local * per_group * DH) + column
        return pltpu.make_async_remote_copy(
            src_ref=obuf.at[pl.ds(row, share), pl.ds(column, width)],
            dst_ref=out_ref.at[:, pl.ds(pl.multiple_of(source, DH), width)],
            send_sem=out_send.at[step, index],
            recv_sem=out_recv.at[step, index],
            device_id={"head": dest},
            device_id_type=MESH,
        )

    def self_copy(column, index):
        row = pl.multiple_of(group * share, share)
        target = group * (kv_local * per_group * DH) + column
        return pltpu.make_async_copy(
            obuf.at[pl.ds(row, share), pl.ds(column, width)],
            out_ref.at[:, pl.ds(pl.multiple_of(target, DH), width)],
            self_sem.at[index],
        )

    def attend(which, h, c):
        row = pl.multiple_of(which * block, block)
        column = pl.multiple_of((h * chunks + c) * width, width)
        key = windows[h, which, :, :DH]
        value = windows[h, which, :, DH:]
        gate = jnp.concatenate([bias[which]] * tile, axis=0)
        for part in range(chunk // tile):
            at = [column + (part * tile + i) * DH for i in range(tile)]
            query = jnp.concatenate(
                [q_buf[pl.ds(row, block), pl.ds(pl.multiple_of(a, DH), DH)] for a in at], axis=0
            )
            scores = gate + lax.dot_general(
                query, key, (((1,), (1,)), ((), ())), preferred_element_type=jnp.float32
            )
            highest = jnp.max(scores, axis=1, keepdims=True)
            expo = jnp.exp2((scores - highest) * factor)
            total = jnp.sum(expo, axis=1, keepdims=True)
            mixed = jnp.dot(
                expo.astype(jnp.bfloat16), value, preferred_element_type=jnp.float32
            )
            mixed = (mixed / total).astype(jnp.bfloat16)
            for i, a in enumerate(at):
                obuf[pl.ds(row, block), pl.ds(pl.multiple_of(a, DH), DH)] = mixed[
                    i * block : (i + 1) * block
                ]
        index = h * chunks + c
        for t in range(dests):
            dest = which * dests + t
            step = lax.rem(dest - group + heads, heads)

            @pl.when(step != 0)
            def _():
                spot = pl.multiple_of(dest * share, share)
                out_copy(step, dest, spot, column, index).start()

            @pl.when(step == 0)
            def _():
                self_copy(column, index).start()

    here = (group * share) // block
    load_q.wait()
    for turn in range(2):
        which = 1 - here if turn == 0 else here
        for h in range(kv_local):
            if turn == 0:
                arrived(h)

            @pl.loop(0, chunks)
            def _(c):
                attend(which, h, c)

    for h in range(kv_local):
        for step in range(1, span + 1):
            up_copy(h, step).wait_send()
            down_copy(h, step).wait_send()
    for index in range(kv_local * chunks):
        column = index * width
        self_copy(column, index).wait()
        for step in range(1, heads):
            dest = lax.rem(group + step, heads)
            spot = pl.multiple_of(dest * share, share)
            out_copy(step, dest, spot, column, index).wait_send()
            sender = lax.rem(group - step + heads, heads)
            target = sender * (kv_local * per_group * DH) + column
            pltpu.make_async_remote_copy(
                src_ref=obuf.at[pl.ds(spot, share), pl.ds(column, width)],
                dst_ref=out_ref.at[:, pl.ds(pl.multiple_of(target, DH), width)],
                send_sem=out_send.at[step, index],
                recv_sem=out_recv.at[step, index],
                device_id={"head": dest},
                device_id_type=MESH,
            ).wait_recv()


def shards(queries, keys, values, lengths, first_block):
    rows_here = queries.shape[0]
    block = rows_here // 2
    kv_local = keys.shape[1] // DH
    per_group = queries.shape[1] // (kv_local * DH)
    pairs = lax.axis_size("ctx")
    heads = lax.axis_size("head")
    span = reach(pairs)
    keys_seen = (span + 1) * block
    chunk = max(per_group // 2, 1)
    tile = max(1, min(chunk, 1024 // keys_seen))
    count = kv_local * (per_group // chunk)
    body = functools.partial(
        kernel, pairs, heads, span, kv_local, per_group, chunk, tile
    )
    hbm = pl.BlockSpec(memory_space=pltpu.HBM)
    return pl.pallas_call(
        body,
        out_shape=jax.ShapeDtypeStruct(
            (rows_here // heads, queries.shape[1] * heads), jnp.bfloat16
        ),
        in_specs=[hbm] * 5,
        out_specs=hbm,
        scratch_shapes=[
            pltpu.SMEM(lengths.shape, jnp.int32),
            pltpu.SMEM(first_block.shape, jnp.int32),
            pltpu.VMEM(keys.shape, jnp.bfloat16),
            pltpu.VMEM(values.shape, jnp.bfloat16),
            pltpu.SemaphoreType.DMA((4,)),
            pltpu.VMEM(queries.shape, jnp.bfloat16),
            pltpu.VMEM((kv_local, rows_here, 2 * DH), jnp.bfloat16),
            pltpu.VMEM((kv_local, span, rows_here, 2 * DH), jnp.bfloat16),
            pltpu.VMEM((kv_local, 2, keys_seen, 2 * DH), jnp.bfloat16),
            pltpu.VMEM((2, block, keys_seen), jnp.float32),
            pltpu.VMEM(queries.shape, jnp.bfloat16),
            pltpu.SemaphoreType.DMA,
            pltpu.SemaphoreType.DMA((kv_local, span)),
            pltpu.SemaphoreType.DMA((kv_local, span)),
            pltpu.SemaphoreType.DMA((kv_local, span)),
            pltpu.SemaphoreType.DMA((kv_local, span)),
            pltpu.SemaphoreType.DMA((heads, count)),
            pltpu.SemaphoreType.DMA((heads, count)),
            pltpu.SemaphoreType.DMA((count,)),
        ],
        compiler_params=pltpu.CompilerParams(
            collective_id=0, has_side_effects=True, vmem_limit_bytes=62 * 2**20
        ),
    )(lengths, first_block, queries, keys, values)


def solution(mesh):
    in_specs = (P("ctx", "head"), P("ctx", "head"), P("ctx", "head"), P(), P())
    out_specs = P(("ctx", "head"), None)
    return jax.shard_map(shards, mesh=mesh, in_specs=in_specs, out_specs=out_specs, check_vma=False)
```

```python
import functools
import math

import jax
import jax.numpy as jnp
from jax import lax
from jax.experimental import pallas as pl
from jax.experimental.pallas import tpu as pltpu
from jax.sharding import PartitionSpec as P

DH = 128
LOWEST = -1e30
MESH = pl.DeviceIdType.MESH


def reach(devices):
    levels = 0
    for power in range(2, 6):
        levels += min(1, devices // 2**power)
    return (1 << levels) - 1


def kernel(
    turned, pairs, heads, span, kv_local, per_group, chunk, tile,
    lengths_hbm, first_hbm, q_hbm, k_hbm, v_hbm, out_ref,
    lengths_ref, first_ref, k_ref, v_ref, in_sem,
    q_buf, own, upper, windows, bias, obuf,
    q_sem, up_send, up_recv, down_send, down_recv, extra_send, out_send, out_recv, self_sem,
):
    device = lax.axis_index("ctx")
    group = lax.axis_index("head")
    rows_here = q_buf.shape[0]
    block = rows_here // 2
    share = rows_here // heads
    dests = block // share
    chunks = per_group // chunk
    width = chunk * DH
    keys_seen = (span + 1) * block

    loads = [
        pltpu.make_async_copy(source, target, in_sem.at[i])
        for i, (source, target) in enumerate(
            [(k_hbm, k_ref), (v_hbm, v_ref), (first_hbm, first_ref), (lengths_hbm, lengths_ref)]
        )
    ]
    for load in loads:
        load.start()
    load_q = pltpu.make_async_copy(q_hbm, q_buf, q_sem)
    load_q.start()

    def around(step):
        return lax.rem(device + (step + pairs), pairs)

    def slot(back):
        return pl.ds((span - back) * block, block)

    fixed = turned is not None
    here = (group * share) // block
    rank = lax.rem(device + turned, pairs) if fixed else device

    def guarded(condition, action):
        if fixed:
            pl.when(condition)(action)
        else:
            action()

    barrier = pltpu.get_barrier_semaphore()

    def greet(step):
        pl.semaphore_signal(barrier, inc=1, device_id={"ctx": around(step)}, device_id_type=MESH)

    for step in range(1, span + 1):
        guarded(rank + step < pairs, functools.partial(greet, step))
        guarded(rank >= step, functools.partial(greet, -step))
    for step in range(1, heads):
        pl.semaphore_signal(
            barrier, inc=1, device_id={"head": lax.rem(group + step, heads)}, device_id_type=MESH
        )
    for load in loads:
        load.wait()
    for h in range(kv_local):
        own[h, :, :DH] = k_ref[:, h * DH : (h + 1) * DH]
        own[h, :, DH:] = v_ref[:, h * DH : (h + 1) * DH]
    if fixed:
        met = jnp.minimum(rank, span) + jnp.minimum(pairs - 1 - rank, span)
        pl.semaphore_wait(barrier, met + heads - 1)
    else:
        pl.semaphore_wait(barrier, 2 * span + heads - 1)

    def up_copy(h, step):
        return pltpu.make_async_remote_copy(
            src_ref=own.at[h, pl.ds(0, block)],
            dst_ref=windows.at[h, 0, slot(step)],
            send_sem=up_send.at[h, step - 1],
            recv_sem=up_recv.at[h, step - 1],
            device_id={"ctx": around(step)},
            device_id_type=MESH,
        )

    def down_copy(h, step):
        if fixed:
            part, target = pl.ds(block, block), windows.at[h, 1, slot(step)]
        else:
            part = pl.ds(0, rows_here) if step < span else pl.ds(block, block)
            target = upper.at[h, step - 1, part]
        return pltpu.make_async_remote_copy(
            src_ref=own.at[h, part],
            dst_ref=target,
            send_sem=down_send.at[h, step - 1],
            recv_sem=down_recv.at[h, step - 1],
            device_id={"ctx": around(-step)},
            device_id_type=MESH,
        )

    extras = [
        (back, away, (2 * pairs - 1 - back + away) // 2)
        for back in range(1, span + 1)
        for away in range(1 - back, back, 2)
        if away != 0
    ]

    def extra_copy(h, index):
        back, away, _ = extras[index]
        return pltpu.make_async_remote_copy(
            src_ref=own.at[h, pl.ds(0, block)],
            dst_ref=windows.at[h, 1, slot(back)],
            send_sem=extra_send.at[h, index],
            recv_sem=down_recv.at[h, back - 1],
            device_id={"ctx": around(-away)},
            device_id_type=MESH,
        )

    def start_ups(h):
        for step in range(span, 0, -1):
            guarded(rank + step < pairs, up_copy(h, step).start)

    def start_downs(h):
        for step in range(span, 0, -1):
            guarded(rank >= step, down_copy(h, step).start)
        if fixed:
            for index, extra in enumerate(extras):
                guarded(rank == extra[2], extra_copy(h, index).start)

    if fixed:

        @pl.when(here == 1)
        def _():
            for h in range(kv_local):
                start_ups(h)
            for h in range(kv_local):
                start_downs(h)

        @pl.when(here == 0)
        def _():
            for h in range(kv_local):
                start_downs(h)
            for h in range(kv_local):
                start_ups(h)

    else:
        for h in range(kv_local):
            start_ups(h)
            start_downs(h)

    first = rank if fixed else first_ref[device]
    shape = (block, keys_seen)
    offset = lax.broadcasted_iota(jnp.int32, shape, 0)
    place = lax.broadcasted_iota(jnp.int32, shape, 1)
    for which in range(2):
        at = first if which == 0 else 2 * pairs - 1 - first
        query_pos = at * block + offset
        key_pos = (at - span) * block + place
        begin = jnp.zeros(shape, jnp.int32)
        end = jnp.int32(0)
        for j in range(lengths_ref.shape[0]):
            end = end + lengths_ref[j]
            ends = jnp.full(shape, end, jnp.int32)
            begin = jnp.where(ends <= query_pos, ends, begin)
        allowed = (key_pos >= begin) & (key_pos <= query_pos)
        bias[which] = jnp.where(allowed, 0.0, LOWEST)
    for h in range(kv_local):
        windows[h, 0, slot(0)] = own[h, :block]
        windows[h, 1, slot(0)] = own[h, block:]
        if fixed:
            for step in range(1, span + 1):

                @pl.when(rank < step)
                def _():
                    windows[h, 0, slot(step)] = jnp.zeros((block, 2 * DH), jnp.bfloat16)

    def landed(which, h):
        def lower():
            for step in range(1, span + 1):
                guarded(rank >= step, up_copy(h, step).wait_recv)

        def higher():
            for step in range(1, span + 1):
                local = (2 * pairs - 1 - step) // 2
                if step % 2 == 1:

                    @pl.when(rank == local)
                    def _():
                        windows[h, 1, slot(step)] = own[h, :block]

                    guarded(rank != local, down_copy(h, step).wait_recv)
                else:
                    down_copy(h, step).wait_recv()

        pl.when(which == 0)(lower)
        pl.when(which == 1)(higher)

    def arrived(h):
        for step in range(1, span + 1):
            up_copy(h, step).wait_recv()
            down_copy(h, step).wait_recv()
        mine = jnp.full((block, 2 * DH), first, jnp.int32)
        for back in range(1, span + 1):
            piece = upper[h, back - 1, block:].astype(jnp.float32)
            for away in range(1 - back, back, 2):
                if away > 0:
                    other = upper[h, away - 1, :block]
                elif away == 0:
                    other = own[h, :block]
                else:
                    other = windows[h, 0, slot(-away)]
                holder = (2 * pairs - 1 - back - away) // 2
                piece = jnp.where(mine == holder, other.astype(jnp.float32), piece)
            windows[h, 1, slot(back)] = piece.astype(jnp.bfloat16)

    factor = math.log2(math.e) / math.sqrt(DH)

    def out_copy(step, dest, row, column, index):
        source = lax.rem(group, heads) * (kv_local * per_group * DH) + column
        return pltpu.make_async_remote_copy(
            src_ref=obuf.at[pl.ds(row, share), pl.ds(column, width)],
            dst_ref=out_ref.at[:, pl.ds(pl.multiple_of(source, DH), width)],
            send_sem=out_send.at[step, index],
            recv_sem=out_recv.at[step, index],
            device_id={"head": dest},
            device_id_type=MESH,
        )

    def self_copy(column, index):
        row = pl.multiple_of(group * share, share)
        target = group * (kv_local * per_group * DH) + column
        return pltpu.make_async_copy(
            obuf.at[pl.ds(row, share), pl.ds(column, width)],
            out_ref.at[:, pl.ds(pl.multiple_of(target, DH), width)],
            self_sem.at[index],
        )

    def attend(which, h, c):
        row = pl.multiple_of(which * block, block)
        column = pl.multiple_of((h * chunks + c) * width, width)
        key = windows[h, which, :, :DH]
        value = windows[h, which, :, DH:]
        gate = jnp.concatenate([bias[which]] * tile, axis=0)
        for part in range(chunk // tile):
            at = [column + (part * tile + i) * DH for i in range(tile)]
            query = jnp.concatenate(
                [q_buf[pl.ds(row, block), pl.ds(pl.multiple_of(a, DH), DH)] for a in at], axis=0
            )
            scores = gate + lax.dot_general(
                query, key, (((1,), (1,)), ((), ())), preferred_element_type=jnp.float32
            )
            highest = jnp.max(scores, axis=1, keepdims=True)
            expo = jnp.exp2((scores - highest) * factor)
            total = jnp.sum(expo, axis=1, keepdims=True)
            mixed = jnp.dot(
                expo.astype(jnp.bfloat16), value, preferred_element_type=jnp.float32
            )
            mixed = (mixed / total).astype(jnp.bfloat16)
            for i, a in enumerate(at):
                obuf[pl.ds(row, block), pl.ds(pl.multiple_of(a, DH), DH)] = mixed[
                    i * block : (i + 1) * block
                ]
        index = h * chunks + c
        for t in range(dests):
            dest = which * dests + t
            step = lax.rem(dest - group + heads, heads)

            @pl.when(step != 0)
            def _():
                spot = pl.multiple_of(dest * share, share)
                out_copy(step, dest, spot, column, index).start()

            @pl.when(step == 0)
            def _():
                self_copy(column, index).start()

    load_q.wait()
    for turn in range(2):
        which = 1 - here if turn == 0 else here
        for h in range(kv_local):
            if fixed:
                landed(which, h)
            elif turn == 0:
                arrived(h)

            @pl.loop(0, chunks)
            def _(c):
                attend(which, h, c)

    for h in range(kv_local):
        for step in range(1, span + 1):
            guarded(rank + step < pairs, up_copy(h, step).wait_send)
            guarded(rank >= step, down_copy(h, step).wait_send)
        if fixed:
            for index, extra in enumerate(extras):
                guarded(rank == extra[2], extra_copy(h, index).wait_send)
    for index in range(kv_local * chunks):
        column = index * width
        self_copy(column, index).wait()
        for step in range(1, heads):
            dest = lax.rem(group + step, heads)
            spot = pl.multiple_of(dest * share, share)
            out_copy(step, dest, spot, column, index).wait_send()
            sender = lax.rem(group - step + heads, heads)
            target = sender * (kv_local * per_group * DH) + column
            pltpu.make_async_remote_copy(
                src_ref=obuf.at[pl.ds(spot, share), pl.ds(column, width)],
                dst_ref=out_ref.at[:, pl.ds(pl.multiple_of(target, DH), width)],
                send_sem=out_send.at[step, index],
                recv_sem=out_recv.at[step, index],
                device_id={"head": dest},
                device_id_type=MESH,
            ).wait_recv()


def shards(queries, keys, values, lengths, first_block):
    rows_here = queries.shape[0]
    block = rows_here // 2
    kv_local = keys.shape[1] // DH
    per_group = queries.shape[1] // (kv_local * DH)
    pairs = lax.axis_size("ctx")
    heads = lax.axis_size("head")
    span = reach(pairs)
    keys_seen = (span + 1) * block
    chunk = max(per_group // 2, 1)
    tile = max(1, min(chunk, 1024 // keys_seen))
    count = kv_local * (per_group // chunk)
    hbm = pl.BlockSpec(memory_space=pltpu.HBM)
    def call(turned):
        return pl.pallas_call(
            functools.partial(
                kernel, turned, pairs, heads, span, kv_local, per_group, chunk, tile
            ),
            out_shape=jax.ShapeDtypeStruct(
                (rows_here // heads, queries.shape[1] * heads), jnp.bfloat16
            ),
            in_specs=[hbm] * 5,
            out_specs=hbm,
            scratch_shapes=[
                pltpu.SMEM(lengths.shape, jnp.int32),
                pltpu.SMEM(first_block.shape, jnp.int32),
                pltpu.VMEM(keys.shape, jnp.bfloat16),
                pltpu.VMEM(values.shape, jnp.bfloat16),
                pltpu.SemaphoreType.DMA((4,)),
                pltpu.VMEM(queries.shape, jnp.bfloat16),
                pltpu.VMEM((kv_local, rows_here, 2 * DH), jnp.bfloat16),
                pltpu.VMEM((kv_local, span, rows_here, 2 * DH), jnp.bfloat16),
                pltpu.VMEM((kv_local, 2, keys_seen, 2 * DH), jnp.bfloat16),
                pltpu.VMEM((2, block, keys_seen), jnp.float32),
                pltpu.VMEM(queries.shape, jnp.bfloat16),
                pltpu.SemaphoreType.DMA,
                pltpu.SemaphoreType.DMA((kv_local, span)),
                pltpu.SemaphoreType.DMA((kv_local, span)),
                pltpu.SemaphoreType.DMA((kv_local, span)),
                pltpu.SemaphoreType.DMA((kv_local, span)),
                pltpu.SemaphoreType.DMA((kv_local, max(1, span * (span - 1)))),
                pltpu.SemaphoreType.DMA((heads, count)),
                pltpu.SemaphoreType.DMA((heads, count)),
                pltpu.SemaphoreType.DMA((count,)),
            ],
            compiler_params=pltpu.CompilerParams(
                collective_id=turned or 0, has_side_effects=True, vmem_limit_bytes=62 * 2**20
            ),
        )

    operands = (lengths, first_block, queries, keys, values)
    if pairs > 8:
        return call(None)(*operands)
    return lax.switch(first_block[0], [call(turned) for turned in range(pairs)], *operands)


def solution(mesh):
    in_specs = (P("ctx", "head"), P("ctx", "head"), P("ctx", "head"), P(), P())
    out_specs = P(("ctx", "head"), None)
    return jax.shard_map(shards, mesh=mesh, in_specs=in_specs, out_specs=out_specs, check_vma=False)
```

```python
import functools
import math

import jax
import jax.numpy as jnp
from jax import lax
from jax.experimental import pallas as pl
from jax.experimental.pallas import tpu as pltpu
from jax.sharding import PartitionSpec as P

DH = 128
LOWEST = -1e30
MESH = pl.DeviceIdType.MESH


def reach(devices):
    levels = 0
    for power in range(2, 6):
        levels += min(1, devices // 2**power)
    return (1 << levels) - 1


def kernel(
    turned, pairs, heads, span, kv_local, per_group, chunk, tile,
    lengths_hbm, first_hbm, q_hbm, k_hbm, v_hbm, out_ref,
    lengths_ref, first_ref, k_ref, v_ref, in_sem,
    q_buf, own, upper, windows, bias, obuf,
    q_sem, up_send, up_recv, down_send, down_recv, extra_send, out_send, out_recv, self_sem,
):
    device = lax.axis_index("ctx")
    group = lax.axis_index("head")
    rows_here = q_buf.shape[0]
    block = rows_here // 2
    share = rows_here // heads
    dests = block // share
    chunks = per_group // chunk
    width = chunk * DH
    keys_seen = (span + 1) * block

    loads = [
        pltpu.make_async_copy(source, target, in_sem.at[i])
        for i, (source, target) in enumerate(
            [(k_hbm, k_ref), (v_hbm, v_ref), (first_hbm, first_ref), (lengths_hbm, lengths_ref)]
        )
    ]
    for load in loads:
        load.start()
    load_q = pltpu.make_async_copy(q_hbm, q_buf, q_sem)
    load_q.start()

    def around(step):
        return lax.rem(device + (step + pairs), pairs)

    def slot(back):
        return pl.ds((span - back) * block, block)

    fixed = turned is not None
    here = (group * share) // block
    rank = lax.rem(device + turned, pairs) if fixed else device

    def guarded(condition, action):
        if fixed:
            pl.when(condition)(action)
        else:
            action()

    barrier = pltpu.get_barrier_semaphore()

    def greet(step):
        pl.semaphore_signal(barrier, inc=1, device_id={"ctx": around(step)}, device_id_type=MESH)

    for step in range(1, span + 1):
        guarded(rank + step < pairs, functools.partial(greet, step))
        guarded(rank >= step, functools.partial(greet, -step))
    for step in range(1, heads):
        pl.semaphore_signal(
            barrier, inc=1, device_id={"head": lax.rem(group + step, heads)}, device_id_type=MESH
        )
    for load in loads:
        load.wait()
    for h in range(kv_local):
        own[h, :, :DH] = k_ref[:, h * DH : (h + 1) * DH]
        own[h, :, DH:] = v_ref[:, h * DH : (h + 1) * DH]
    if fixed:
        met = jnp.minimum(rank, span) + jnp.minimum(pairs - 1 - rank, span)
        pl.semaphore_wait(barrier, met + heads - 1)
    else:
        pl.semaphore_wait(barrier, 2 * span + heads - 1)

    def up_copy(h, step):
        return pltpu.make_async_remote_copy(
            src_ref=own.at[h, pl.ds(0, block)],
            dst_ref=windows.at[h, 0, slot(step)],
            send_sem=up_send.at[h, step - 1],
            recv_sem=up_recv.at[h, step - 1],
            device_id={"ctx": around(step)},
            device_id_type=MESH,
        )

    def down_copy(h, step):
        if fixed:
            part, target = pl.ds(block, block), windows.at[h, 1, slot(step)]
        else:
            part = pl.ds(0, rows_here) if step < span else pl.ds(block, block)
            target = upper.at[h, step - 1, part]
        return pltpu.make_async_remote_copy(
            src_ref=own.at[h, part],
            dst_ref=target,
            send_sem=down_send.at[h, step - 1],
            recv_sem=down_recv.at[h, step - 1],
            device_id={"ctx": around(-step)},
            device_id_type=MESH,
        )

    extras = [
        (back, away, (2 * pairs - 1 - back + away) // 2)
        for back in range(1, span + 1)
        for away in range(1 - back, back, 2)
        if away != 0
    ]

    def extra_copy(h, index):
        back, away, _ = extras[index]
        return pltpu.make_async_remote_copy(
            src_ref=own.at[h, pl.ds(0, block)],
            dst_ref=windows.at[h, 1, slot(back)],
            send_sem=extra_send.at[h, index],
            recv_sem=down_recv.at[h, back - 1],
            device_id={"ctx": around(-away)},
            device_id_type=MESH,
        )

    def start_ups(h):
        for step in range(span, 0, -1):
            guarded(rank + step < pairs, up_copy(h, step).start)

    def start_downs(h):
        for step in range(span, 0, -1):
            guarded(rank >= step, down_copy(h, step).start)
        if fixed:
            for index, extra in enumerate(extras):
                guarded(rank == extra[2], extra_copy(h, index).start)

    if fixed:

        @pl.loop(0, 2 * kv_local)
        def _(n):
            h = lax.rem(n, kv_local)
            upward = (n < kv_local) == (here == 1)
            pl.when(upward)(functools.partial(start_ups, h))
            pl.when(jnp.logical_not(upward))(functools.partial(start_downs, h))

    else:

        @pl.loop(0, kv_local)
        def _(h):
            start_ups(h)
            start_downs(h)

    first = rank if fixed else first_ref[device]
    shape = (block, keys_seen)
    offset = lax.broadcasted_iota(jnp.int32, shape, 0)
    place = lax.broadcasted_iota(jnp.int32, shape, 1)
    for which in range(2):
        at = first if which == 0 else 2 * pairs - 1 - first
        query_pos = at * block + offset
        key_pos = (at - span) * block + place
        begin = jnp.zeros(shape, jnp.int32)
        end = jnp.int32(0)
        for j in range(lengths_ref.shape[0]):
            end = end + lengths_ref[j]
            ends = jnp.full(shape, end, jnp.int32)
            begin = jnp.where(ends <= query_pos, ends, begin)
        allowed = (key_pos >= begin) & (key_pos <= query_pos)
        bias[which] = jnp.where(allowed, 0.0, LOWEST)
    for h in range(kv_local):
        windows[h, 0, slot(0)] = own[h, :block]
        windows[h, 1, slot(0)] = own[h, block:]
        if fixed:
            for step in range(1, span + 1):

                @pl.when(rank < step)
                def _():
                    windows[h, 0, slot(step)] = jnp.zeros((block, 2 * DH), jnp.bfloat16)

    def landed(which, h):
        def lower():
            for step in range(1, span + 1):
                guarded(rank >= step, up_copy(h, step).wait_recv)

        def higher():
            for step in range(1, span + 1):
                local = (2 * pairs - 1 - step) // 2
                if step % 2 == 1:

                    @pl.when(rank == local)
                    def _():
                        windows[h, 1, slot(step)] = own[h, :block]

                    guarded(rank != local, down_copy(h, step).wait_recv)
                else:
                    down_copy(h, step).wait_recv()

        pl.when(which == 0)(lower)
        pl.when(which == 1)(higher)

    def arrived(h):
        for step in range(1, span + 1):
            up_copy(h, step).wait_recv()
            down_copy(h, step).wait_recv()
        mine = jnp.full((block, 2 * DH), first, jnp.int32)
        for back in range(1, span + 1):
            piece = upper[h, back - 1, block:].astype(jnp.float32)
            for away in range(1 - back, back, 2):
                if away > 0:
                    other = upper[h, away - 1, :block]
                elif away == 0:
                    other = own[h, :block]
                else:
                    other = windows[h, 0, slot(-away)]
                holder = (2 * pairs - 1 - back - away) // 2
                piece = jnp.where(mine == holder, other.astype(jnp.float32), piece)
            windows[h, 1, slot(back)] = piece.astype(jnp.bfloat16)

    factor = math.log2(math.e) / math.sqrt(DH)

    def out_copy(step, dest, row, column, index):
        source = lax.rem(group, heads) * (kv_local * per_group * DH) + column
        return pltpu.make_async_remote_copy(
            src_ref=obuf.at[pl.ds(row, share), pl.ds(column, width)],
            dst_ref=out_ref.at[:, pl.ds(pl.multiple_of(source, DH), width)],
            send_sem=out_send.at[step, index],
            recv_sem=out_recv.at[step, index],
            device_id={"head": dest},
            device_id_type=MESH,
        )

    def self_copy(column, index):
        row = pl.multiple_of(group * share, share)
        target = group * (kv_local * per_group * DH) + column
        return pltpu.make_async_copy(
            obuf.at[pl.ds(row, share), pl.ds(column, width)],
            out_ref.at[:, pl.ds(pl.multiple_of(target, DH), width)],
            self_sem.at[index],
        )

    def attend(which, h, c):
        row = pl.multiple_of(which * block, block)
        column = pl.multiple_of((h * chunks + c) * width, width)
        key = windows[h, which, :, :DH]
        value = windows[h, which, :, DH:]
        gate = jnp.concatenate([bias[which]] * tile, axis=0)
        for part in range(chunk // tile):
            at = [column + (part * tile + i) * DH for i in range(tile)]
            query = jnp.concatenate(
                [q_buf[pl.ds(row, block), pl.ds(pl.multiple_of(a, DH), DH)] for a in at], axis=0
            )
            scores = gate + lax.dot_general(
                query, key, (((1,), (1,)), ((), ())), preferred_element_type=jnp.float32
            )
            highest = jnp.max(scores, axis=1, keepdims=True)
            expo = jnp.exp2((scores - highest) * factor)
            total = jnp.sum(expo, axis=1, keepdims=True)
            mixed = jnp.dot(
                expo.astype(jnp.bfloat16), value, preferred_element_type=jnp.float32
            )
            mixed = (mixed / total).astype(jnp.bfloat16)
            for i, a in enumerate(at):
                obuf[pl.ds(row, block), pl.ds(pl.multiple_of(a, DH), DH)] = mixed[
                    i * block : (i + 1) * block
                ]
        index = h * chunks + c
        for t in range(dests):
            dest = which * dests + t
            step = lax.rem(dest - group + heads, heads)

            @pl.when(step != 0)
            def _():
                spot = pl.multiple_of(dest * share, share)
                out_copy(step, dest, spot, column, index).start()

            @pl.when(step == 0)
            def _():
                self_copy(column, index).start()

    load_q.wait()
    count = kv_local * chunks

    @pl.loop(0, 2 * count)
    def _(n):
        turn = n // count
        which = jnp.where(turn == 0, 1 - here, here)
        h = lax.rem(n, count) // chunks
        c = lax.rem(n, chunks)
        if fixed:
            pl.when(c == 0)(functools.partial(landed, which, h))
        else:
            pl.when((c == 0) & (turn == 0))(functools.partial(arrived, h))
        attend(which, h, c)

    @pl.loop(0, kv_local)
    def _(h):
        for step in range(1, span + 1):
            guarded(rank + step < pairs, up_copy(h, step).wait_send)
            guarded(rank >= step, down_copy(h, step).wait_send)
        if fixed:
            for index, extra in enumerate(extras):
                guarded(rank == extra[2], extra_copy(h, index).wait_send)

    @pl.loop(0, count)
    def _(index):
        column = pl.multiple_of(index * width, width)
        self_copy(column, index).wait()
        for step in range(1, heads):
            dest = lax.rem(group + step, heads)
            spot = pl.multiple_of(dest * share, share)
            out_copy(step, dest, spot, column, index).wait_send()
            sender = lax.rem(group - step + heads, heads)
            target = sender * (kv_local * per_group * DH) + column
            pltpu.make_async_remote_copy(
                src_ref=obuf.at[pl.ds(spot, share), pl.ds(column, width)],
                dst_ref=out_ref.at[:, pl.ds(pl.multiple_of(target, DH), width)],
                send_sem=out_send.at[step, index],
                recv_sem=out_recv.at[step, index],
                device_id={"head": dest},
                device_id_type=MESH,
            ).wait_recv()


def shards(queries, keys, values, lengths, first_block):
    rows_here = queries.shape[0]
    block = rows_here // 2
    kv_local = keys.shape[1] // DH
    per_group = queries.shape[1] // (kv_local * DH)
    pairs = lax.axis_size("ctx")
    heads = lax.axis_size("head")
    span = reach(pairs)
    keys_seen = (span + 1) * block
    chunk = max(per_group // 2, 1)
    tile = max(1, min(chunk, 1024 // keys_seen))
    count = kv_local * (per_group // chunk)
    hbm = pl.BlockSpec(memory_space=pltpu.HBM)
    def call(turned):
        return pl.pallas_call(
            functools.partial(
                kernel, turned, pairs, heads, span, kv_local, per_group, chunk, tile
            ),
            out_shape=jax.ShapeDtypeStruct(
                (rows_here // heads, queries.shape[1] * heads), jnp.bfloat16
            ),
            in_specs=[hbm] * 5,
            out_specs=hbm,
            scratch_shapes=[
                pltpu.SMEM(lengths.shape, jnp.int32),
                pltpu.SMEM(first_block.shape, jnp.int32),
                pltpu.VMEM(keys.shape, jnp.bfloat16),
                pltpu.VMEM(values.shape, jnp.bfloat16),
                pltpu.SemaphoreType.DMA((4,)),
                pltpu.VMEM(queries.shape, jnp.bfloat16),
                pltpu.VMEM((kv_local, rows_here, 2 * DH), jnp.bfloat16),
                pltpu.VMEM((kv_local, span, rows_here, 2 * DH), jnp.bfloat16),
                pltpu.VMEM((kv_local, 2, keys_seen, 2 * DH), jnp.bfloat16),
                pltpu.VMEM((2, block, keys_seen), jnp.float32),
                pltpu.VMEM(queries.shape, jnp.bfloat16),
                pltpu.SemaphoreType.DMA,
                pltpu.SemaphoreType.DMA((kv_local, span)),
                pltpu.SemaphoreType.DMA((kv_local, span)),
                pltpu.SemaphoreType.DMA((kv_local, span)),
                pltpu.SemaphoreType.DMA((kv_local, span)),
                pltpu.SemaphoreType.DMA((kv_local, max(1, span * (span - 1)))),
                pltpu.SemaphoreType.DMA((heads, count)),
                pltpu.SemaphoreType.DMA((heads, count)),
                pltpu.SemaphoreType.DMA((count,)),
            ],
            compiler_params=pltpu.CompilerParams(
                collective_id=turned or 0, has_side_effects=True, vmem_limit_bytes=62 * 2**20
            ),
        )

    operands = (lengths, first_block, queries, keys, values)
    if pairs > 8:
        return call(None)(*operands)
    return lax.switch(first_block[0], [call(turned) for turned in range(pairs)], *operands)


def solution(mesh):
    in_specs = (P("ctx", "head"), P("ctx", "head"), P("ctx", "head"), P(), P())
    out_specs = P(("ctx", "head"), None)
    return jax.shard_map(shards, mesh=mesh, in_specs=in_specs, out_specs=out_specs, check_vma=False)
```

```python
import functools
import math

import jax
import jax.numpy as jnp
from jax import lax
from jax.experimental import pallas as pl
from jax.experimental.pallas import tpu as pltpu
from jax.sharding import PartitionSpec as P

DH = 128
LOWEST = -1e30
MESH = pl.DeviceIdType.MESH


def reach(devices):
    levels = 0
    for power in range(2, 6):
        levels += min(1, devices // 2**power)
    return (1 << levels) - 1


def kernel(
    turned, pairs, heads, span, kv_local, per_group, chunk, tile,
    lengths_hbm, first_hbm, q_hbm, k_hbm, v_hbm, out_ref,
    lengths_ref, first_ref, k_ref, v_ref, in_sem,
    q_buf, own, upper, windows, bias, obuf,
    q_sem, up_send, up_recv, down_send, down_recv, extra_send, out_send, out_recv, self_sem,
):
    device = lax.axis_index("ctx")
    group = lax.axis_index("head")
    rows_here = q_buf.shape[0]
    block = rows_here // 2
    share = rows_here // heads
    dests = block // share
    chunks = per_group // chunk
    width = chunk * DH
    keys_seen = (span + 1) * block

    loads = [
        pltpu.make_async_copy(source, target, in_sem.at[i])
        for i, (source, target) in enumerate(
            [(k_hbm, k_ref), (v_hbm, v_ref), (first_hbm, first_ref), (lengths_hbm, lengths_ref)]
        )
    ]
    for load in loads:
        load.start()
    load_q = pltpu.make_async_copy(q_hbm, q_buf, q_sem)
    load_q.start()

    def around(step):
        return lax.rem(device + (step + pairs), pairs)

    def slot(back):
        return pl.ds((span - back) * block, block)

    fixed = turned is not None
    here = (group * share) // block
    rank = lax.rem(device + turned, pairs) if fixed else device

    def guarded(condition, action):
        if fixed:
            pl.when(condition)(action)
        else:
            action()

    barrier = pltpu.get_barrier_semaphore()

    def greet(step):
        pl.semaphore_signal(barrier, inc=1, device_id={"ctx": around(step)}, device_id_type=MESH)

    for step in range(1, span + 1):
        guarded(rank + step < pairs, functools.partial(greet, step))
        guarded(rank >= step, functools.partial(greet, -step))
    for step in range(1, heads):
        pl.semaphore_signal(
            barrier, inc=1, device_id={"head": lax.rem(group + step, heads)}, device_id_type=MESH
        )
    for load in loads:
        load.wait()
    for h in range(kv_local):
        own[h, :, :DH] = k_ref[:, h * DH : (h + 1) * DH]
        own[h, :, DH:] = v_ref[:, h * DH : (h + 1) * DH]
    if fixed:
        met = jnp.minimum(rank, span) + jnp.minimum(pairs - 1 - rank, span)
        pl.semaphore_wait(barrier, met + heads - 1)
    else:
        pl.semaphore_wait(barrier, 2 * span + heads - 1)

    def up_copy(h, step):
        return pltpu.make_async_remote_copy(
            src_ref=own.at[h, pl.ds(0, block)],
            dst_ref=windows.at[h, 0, slot(step)],
            send_sem=up_send.at[h, step - 1],
            recv_sem=up_recv.at[h, step - 1],
            device_id={"ctx": around(step)},
            device_id_type=MESH,
        )

    def down_copy(h, step):
        if fixed:
            part, target = pl.ds(block, block), windows.at[h, 1, slot(step)]
        else:
            part = pl.ds(0, rows_here) if step < span else pl.ds(block, block)
            target = upper.at[h, step - 1, part]
        return pltpu.make_async_remote_copy(
            src_ref=own.at[h, part],
            dst_ref=target,
            send_sem=down_send.at[h, step - 1],
            recv_sem=down_recv.at[h, step - 1],
            device_id={"ctx": around(-step)},
            device_id_type=MESH,
        )

    extras = [
        (back, away, (2 * pairs - 1 - back + away) // 2)
        for back in range(1, span + 1)
        for away in range(1 - back, back, 2)
        if away != 0
    ]

    def extra_copy(h, index):
        back, away, _ = extras[index]
        return pltpu.make_async_remote_copy(
            src_ref=own.at[h, pl.ds(0, block)],
            dst_ref=windows.at[h, 1, slot(back)],
            send_sem=extra_send.at[h, index],
            recv_sem=down_recv.at[h, back - 1],
            device_id={"ctx": around(-away)},
            device_id_type=MESH,
        )

    def start_ups(h):
        for step in range(span, 0, -1):
            guarded(rank + step < pairs, up_copy(h, step).start)

    def start_downs(h):
        for step in range(span, 0, -1):
            guarded(rank >= step, down_copy(h, step).start)
        if fixed:
            for index, extra in enumerate(extras):
                guarded(rank == extra[2], extra_copy(h, index).start)

    if fixed:

        @pl.loop(0, 2 * kv_local)
        def _(n):
            h = lax.rem(n, kv_local)
            upward = (n < kv_local) == (here == 1)
            pl.when(upward)(functools.partial(start_ups, h))
            pl.when(jnp.logical_not(upward))(functools.partial(start_downs, h))

    else:

        @pl.loop(0, kv_local)
        def _(h):
            start_ups(h)
            start_downs(h)

    first = rank if fixed else first_ref[device]
    shape = (block, keys_seen)
    offset = lax.broadcasted_iota(jnp.int32, shape, 0)
    place = lax.broadcasted_iota(jnp.int32, shape, 1)
    for which in range(2):
        at = first if which == 0 else 2 * pairs - 1 - first
        query_pos = at * block + offset
        key_pos = (at - span) * block + place
        begin = jnp.zeros(shape, jnp.int32)
        end = jnp.int32(0)
        for j in range(lengths_ref.shape[0]):
            end = end + lengths_ref[j]
            ends = jnp.full(shape, end, jnp.int32)
            begin = jnp.where(ends <= query_pos, ends, begin)
        allowed = (key_pos >= begin) & (key_pos <= query_pos)
        bias[which] = jnp.where(allowed, 0.0, LOWEST)
    for h in range(kv_local):
        windows[h, 0, slot(0)] = own[h, :block]
        windows[h, 1, slot(0)] = own[h, block:]
        if fixed:
            for step in range(1, span + 1):

                @pl.when(rank < step)
                def _():
                    windows[h, 0, slot(step)] = jnp.zeros((block, 2 * DH), jnp.bfloat16)

    def landed(which, h):
        def lower():
            for step in range(1, span + 1):
                guarded(rank >= step, up_copy(h, step).wait_recv)

        def higher():
            for step in range(1, span + 1):
                local = (2 * pairs - 1 - step) // 2
                if step % 2 == 1:

                    @pl.when(rank == local)
                    def _():
                        windows[h, 1, slot(step)] = own[h, :block]

                    guarded(rank != local, down_copy(h, step).wait_recv)
                else:
                    down_copy(h, step).wait_recv()

        pl.when(which == 0)(lower)
        pl.when(which == 1)(higher)

    def arrived(h):
        for step in range(1, span + 1):
            up_copy(h, step).wait_recv()
            down_copy(h, step).wait_recv()
        mine = jnp.full((block, 2 * DH), first, jnp.int32)
        for back in range(1, span + 1):
            piece = upper[h, back - 1, block:].astype(jnp.float32)
            for away in range(1 - back, back, 2):
                if away > 0:
                    other = upper[h, away - 1, :block]
                elif away == 0:
                    other = own[h, :block]
                else:
                    other = windows[h, 0, slot(-away)]
                holder = (2 * pairs - 1 - back - away) // 2
                piece = jnp.where(mine == holder, other.astype(jnp.float32), piece)
            windows[h, 1, slot(back)] = piece.astype(jnp.bfloat16)

    factor = math.log2(math.e) / math.sqrt(DH)

    def out_copy(step, dest, row, column, index):
        source = lax.rem(group, heads) * (kv_local * per_group * DH) + column
        return pltpu.make_async_remote_copy(
            src_ref=obuf.at[pl.ds(row, share), pl.ds(column, width)],
            dst_ref=out_ref.at[:, pl.ds(pl.multiple_of(source, DH), width)],
            send_sem=out_send.at[step, index],
            recv_sem=out_recv.at[step, index],
            device_id={"head": dest},
            device_id_type=MESH,
        )

    def self_copy(column, index):
        row = pl.multiple_of(group * share, share)
        target = group * (kv_local * per_group * DH) + column
        return pltpu.make_async_copy(
            obuf.at[pl.ds(row, share), pl.ds(column, width)],
            out_ref.at[:, pl.ds(pl.multiple_of(target, DH), width)],
            self_sem.at[index],
        )

    def attend(which, h, c):
        row = pl.multiple_of(which * block, block)
        column = pl.multiple_of((h * chunks + c) * width, width)
        key = windows[h, which, :, :DH]
        value = windows[h, which, :, DH:]
        gate = jnp.concatenate([bias[which]] * tile, axis=0)
        for part in range(chunk // tile):
            at = [column + (part * tile + i) * DH for i in range(tile)]
            query = jnp.concatenate(
                [q_buf[pl.ds(row, block), pl.ds(pl.multiple_of(a, DH), DH)] for a in at], axis=0
            )
            scores = gate + lax.dot_general(
                query, key, (((1,), (1,)), ((), ())), preferred_element_type=jnp.float32
            )
            highest = jnp.max(scores, axis=1, keepdims=True)
            expo = jnp.exp2((scores - highest) * factor)
            total = jnp.sum(expo, axis=1, keepdims=True)
            mixed = jnp.dot(
                expo.astype(jnp.bfloat16), value, preferred_element_type=jnp.float32
            )
            mixed = (mixed / total).astype(jnp.bfloat16)
            for i, a in enumerate(at):
                obuf[pl.ds(row, block), pl.ds(pl.multiple_of(a, DH), DH)] = mixed[
                    i * block : (i + 1) * block
                ]
        index = h * chunks + c
        for t in range(dests):
            dest = which * dests + t
            step = lax.rem(dest - group + heads, heads)

            @pl.when(step != 0)
            def _():
                spot = pl.multiple_of(dest * share, share)
                out_copy(step, dest, spot, column, index).start()

            @pl.when(step == 0)
            def _():
                self_copy(column, index).start()

    load_q.wait()
    count = kv_local * chunks

    @pl.loop(0, 2 * count)
    def _(n):
        turn = n // count
        which = jnp.where(turn == 0, 1 - here, here)
        h = lax.rem(n, count) // chunks
        c = lax.rem(n, chunks)
        if fixed:
            pl.when(c == 0)(functools.partial(landed, which, h))
        else:
            pl.when((c == 0) & (turn == 0))(functools.partial(arrived, h))
        attend(which, h, c)

    @pl.loop(0, kv_local)
    def _(h):
        for step in range(1, span + 1):
            guarded(rank + step < pairs, up_copy(h, step).wait_send)
            guarded(rank >= step, down_copy(h, step).wait_send)
        if fixed:
            for index, extra in enumerate(extras):
                guarded(rank == extra[2], extra_copy(h, index).wait_send)

    @pl.loop(0, count)
    def _(index):
        column = pl.multiple_of(index * width, width)
        self_copy(column, index).wait()
        for step in range(1, heads):
            dest = lax.rem(group + step, heads)
            spot = pl.multiple_of(dest * share, share)
            out_copy(step, dest, spot, column, index).wait_send()
            sender = lax.rem(group - step + heads, heads)
            target = sender * (kv_local * per_group * DH) + column
            pltpu.make_async_remote_copy(
                src_ref=obuf.at[pl.ds(spot, share), pl.ds(column, width)],
                dst_ref=out_ref.at[:, pl.ds(pl.multiple_of(target, DH), width)],
                send_sem=out_send.at[step, index],
                recv_sem=out_recv.at[step, index],
                device_id={"head": dest},
                device_id_type=MESH,
            ).wait_recv()


def shards(queries, keys, values, lengths, first_block):
    rows_here = queries.shape[0]
    block = rows_here // 2
    kv_local = keys.shape[1] // DH
    per_group = queries.shape[1] // (kv_local * DH)
    pairs = lax.axis_size("ctx")
    heads = lax.axis_size("head")
    span = reach(pairs)
    keys_seen = (span + 1) * block
    chunk = max(per_group // 4, 1)
    tile = max(1, min(chunk, 1024 // keys_seen))
    count = kv_local * (per_group // chunk)
    hbm = pl.BlockSpec(memory_space=pltpu.HBM)
    def call(turned):
        return pl.pallas_call(
            functools.partial(
                kernel, turned, pairs, heads, span, kv_local, per_group, chunk, tile
            ),
            out_shape=jax.ShapeDtypeStruct(
                (rows_here // heads, queries.shape[1] * heads), jnp.bfloat16
            ),
            in_specs=[hbm] * 5,
            out_specs=hbm,
            scratch_shapes=[
                pltpu.SMEM(lengths.shape, jnp.int32),
                pltpu.SMEM(first_block.shape, jnp.int32),
                pltpu.VMEM(keys.shape, jnp.bfloat16),
                pltpu.VMEM(values.shape, jnp.bfloat16),
                pltpu.SemaphoreType.DMA((4,)),
                pltpu.VMEM(queries.shape, jnp.bfloat16),
                pltpu.VMEM((kv_local, rows_here, 2 * DH), jnp.bfloat16),
                pltpu.VMEM((kv_local, span, rows_here, 2 * DH), jnp.bfloat16),
                pltpu.VMEM((kv_local, 2, keys_seen, 2 * DH), jnp.bfloat16),
                pltpu.VMEM((2, block, keys_seen), jnp.float32),
                pltpu.VMEM(queries.shape, jnp.bfloat16),
                pltpu.SemaphoreType.DMA,
                pltpu.SemaphoreType.DMA((kv_local, span)),
                pltpu.SemaphoreType.DMA((kv_local, span)),
                pltpu.SemaphoreType.DMA((kv_local, span)),
                pltpu.SemaphoreType.DMA((kv_local, span)),
                pltpu.SemaphoreType.DMA((kv_local, max(1, span * (span - 1)))),
                pltpu.SemaphoreType.DMA((heads, count)),
                pltpu.SemaphoreType.DMA((heads, count)),
                pltpu.SemaphoreType.DMA((count,)),
            ],
            compiler_params=pltpu.CompilerParams(
                collective_id=turned or 0, has_side_effects=True, vmem_limit_bytes=62 * 2**20
            ),
        )

    operands = (lengths, first_block, queries, keys, values)
    if pairs > 8:
        return call(None)(*operands)
    return lax.switch(first_block[0], [call(turned) for turned in range(pairs)], *operands)


def solution(mesh):
    in_specs = (P("ctx", "head"), P("ctx", "head"), P("ctx", "head"), P(), P())
    out_specs = P(("ctx", "head"), None)
    return jax.shard_map(shards, mesh=mesh, in_specs=in_specs, out_specs=out_specs, check_vma=False)
```
